128 devices in a mesh: member: 2 (over y_hi), tile: 64 (over z, y_lo, x, core).
Axes of the slice: x: 4, y: 4 (y_hi: 2, y_lo: 2; y = y_hi * 2 + y_lo), z: 4, core: 2. Of those that a mesh axis runs over, the one named last changes fastest.
Arguments:
- vectors: float32 [4, 3, 8, 2048, 512], P('member', None, None, 'tile'), may hold values from -6 to 6
- trajectory: bfloat16 [4, 3, 8, 2048, 512], P('member', None, None, 'tile'), may hold values from -1 to 1
- slot_table: int32 [4], replicated, may hold values from 0 to 3, each once
Outputs:
- advanced: float32 [4, 3, 8, 2048, 512], P('member', None, None, 'tile')
The draws below stay inside these ranges and needn't reach their ends.
Inputs may be any that keep to these rules, and one draw needn't show every extreme that they name: `slot_table`: each slot appears once; slot g lies on member index g // 2.
All inputs are finite; a program needn't handle non-finite values.
Results may differ from the reference program's by a relative error of at most 0.0003.
Values may be sent and summed in bfloat16 or wider, within the bound.
No kernel may reach another device: no remote copies, remote signals or barrier semaphores. Data moves between devices by JAX's collectives and lax.ppermute only.
A program may use at most 128 MiB of HBM per device.

```python
import jax
import jax.numpy as jnp

NLAT = 512
LEV = 8
STEPS = 4
VECS = 4
NLON = 2048


def steps_of(key, extent, cuts, low, top_value):
    gain, own = 1.0, jax.random.fold_in(key, 6)
    for axis_at, blocks in cuts:
        draws = jnp.exp(jax.random.uniform(jax.random.fold_in(own, axis_at), (blocks,), jnp.float32, low / len(cuts), top_value / len(cuts)))
        gain = gain * jnp.repeat(draws, extent[axis_at] // blocks).reshape([-1 if axis == axis_at else 1 for axis in range(len(extent))])
    return gain


def noise(rng, extent, scale, limit, shards=(), held_as=jnp.bfloat16):
    array = scale * jax.random.normal(rng, extent, jnp.float32)
    if shards:
        array = array * steps_of(rng, extent, shards, -0.22, 0.18)
    return jnp.clip(array, -limit, limit).astype(held_as)


def setup_inputs(seed: int = 0) -> dict:
    splits = jax.random.split(jax.random.key(seed), 4)
    vectors = noise(splits[0], (VECS, 3, LEV, NLON, NLAT), 1.0, 6.0, ((0, 2), (3, 64)), jnp.float32)
    trajectory = jnp.clip(jax.random.uniform(splits[1], (STEPS, 3, LEV, NLON, NLAT), jnp.float32, -1.0, 1.0) * steps_of(splits[1], (STEPS, 3, LEV, NLON, NLAT), ((0, 2), (3, 64)), -0.4, 0.0), -1.0, 1.0).astype(jnp.bfloat16)
    slot_table = jax.random.permutation(splits[2], STEPS).astype(jnp.int32)
    return {"vectors": vectors, "trajectory": trajectory, "slot_table": slot_table}


COURANT = 0.8


def lon_deriv(padded):
    return (8.0 * (padded[..., 3:-1, :] - padded[..., 1:-3, :]) - (padded[..., 4:, :] - padded[..., :-4, :])) / 12.0


def lat_deriv(field):
    widths = [(0, 0)] * (field.ndim - 1) + [(1, 1)]
    padded = jnp.pad(field, widths)
    return (padded[..., 2:] - padded[..., :-2]) * 0.5


def wrap_lon(field):
    widths = [(0, 0)] * (field.ndim - 2) + [(2, 2), (0, 0)]
    return jnp.pad(field, widths, mode="wrap")


def tendency(pert, base, base_dx, base_dy):
    wind_u = base[0][None, None]
    wind_v = base[1][None, None]
    advect = wind_u * lon_deriv(wrap_lon(pert)) + wind_v * lat_deriv(pert)
    forcing = pert[:, 0:1] * base_dx[None] + pert[:, 1:2] * base_dy[None]
    return -COURANT * (advect + forcing)


def reference(vectors, trajectory, slot_table):
    pert = vectors
    for step in range(STEPS):
        base = trajectory[slot_table[step]].astype(jnp.float32)
        base_dx = lon_deriv(wrap_lon(base))
        base_dy = lat_deriv(base)
        first = pert + tendency(pert, base, base_dx, base_dy)
        second = 0.75 * pert + 0.25 * (first + tendency(first, base, base_dx, base_dy))
        pert = pert / 3.0 + (2.0 / 3.0) * (second + tendency(second, base, base_dx, base_dy))
    return pert
```

```python
import functools

import jax
import jax.numpy as jnp
import numpy as np
from jax import lax
from jax.experimental import pallas as pl
from jax.experimental.pallas import tpu as pltpu
from jax.sharding import PartitionSpec as P

STEPS = 4
COURANT = 0.8
NK, LANES, LEV, LON, NLAT = 4, 128, 8, 32, 512
CORE = LON * LEV
WIDE = 6
RIM = WIDE * LEV
NEAR = 2 * LEV
EXT = CORE + 2 * RIM
VMEM_LIMIT = 48 * 1024 * 1024
F32, BF16 = jnp.float32, jnp.bfloat16


def lane_order():
    order = np.zeros((NLAT, NLAT), np.float32)
    for lat in range(NLAT):
        order[lat, (lat % NK) * LANES + lat // NK] = 1.0
    return order


def dot(a, b):
    return jnp.dot(a, b, preferred_element_type=F32)


def split_dot(x, order):
    high = x.astype(BF16)
    rest = (x - high.astype(F32)).astype(BF16)
    return dot(high, order) + dot(rest, order)


def scatter_rows(y, dst):
    for lev in range(LEV):
        for tile in range(LON // 8):
            for k in range(NK):
                dst[k, pl.ds(tile * 64 + lev, 8, stride=LEV), :] = y[
                    lev * LON + tile * 8 : lev * LON + tile * 8 + 8, k * LANES : (k + 1) * LANES
                ]


def gather_rows(src):
    rows = []
    for lev in range(LEV):
        for tile in range(LON // 8):
            rows.append(
                jnp.concatenate([src[k, pl.ds(tile * 64 + lev, 8, stride=LEV), :] for k in range(NK)], axis=1)
            )
    return jnp.concatenate(rows, axis=0)


def pack_edges(p, head_ref, tail_ref, at):
    for k in range(NK):
        head = p[k, pl.ds(0, RIM), :]
        tail = p[k, pl.ds(CORE - RIM, RIM), :]
        high, last = head.astype(BF16), tail.astype(BF16)
        head_ref[(*at, k, pl.ds(0, RIM), slice(None))] = high
        head_ref[(*at, k, pl.ds(RIM, NEAR), slice(None))] = (head[:NEAR] - high[:NEAR].astype(F32)).astype(BF16)
        tail_ref[(*at, k, pl.ds(0, RIM), slice(None))] = last
        tail_ref[(*at, k, pl.ds(RIM, NEAR), slice(None))] = (tail[RIM - NEAR :] - last[RIM - NEAR :].astype(F32)).astype(BF16)


def base_kernel(slot_ref, traj_ref, order_ref, core_ref, head_ref, tail_ref, rows):
    y = dot(traj_ref[0, 0].reshape(LEV * LON, NLAT), order_ref[...])
    scatter_rows(y, rows)
    for k in range(NK):
        core_ref[0, k] = rows[k].astype(BF16)
        head_ref[0, k] = rows[k, pl.ds(0, RIM), :].astype(BF16)
        tail_ref[0, k] = rows[k, pl.ds(CORE - RIM, RIM), :].astype(BF16)


def convert_base(slot, trajectory, order):
    spec = pltpu.PrefetchScalarGridSpec(
        num_scalar_prefetch=1,
        grid=(3,),
        in_specs=[
            pl.BlockSpec((1, 1, LEV, LON, NLAT), lambda c, slot: (slot[0], c, 0, 0, 0)),
            pl.BlockSpec((NLAT, NLAT), lambda c, slot: (0, 0)),
        ],
        out_specs=[
            pl.BlockSpec((1, NK, CORE, LANES), lambda c, slot: (c, 0, 0, 0)),
            pl.BlockSpec((1, NK, RIM, LANES), lambda c, slot: (c, 0, 0, 0)),
            pl.BlockSpec((1, NK, RIM, LANES), lambda c, slot: (c, 0, 0, 0)),
        ],
        scratch_shapes=[pltpu.VMEM((NK, CORE, LANES), F32)],
    )
    return pl.pallas_call(
        base_kernel,
        grid_spec=spec,
        out_shape=[
            jax.ShapeDtypeStruct((3, NK, CORE, LANES), BF16),
            jax.ShapeDtypeStruct((3, NK, RIM, LANES), BF16),
            jax.ShapeDtypeStruct((3, NK, RIM, LANES), BF16),
        ],
        compiler_params=pltpu.CompilerParams(vmem_limit_bytes=VMEM_LIMIT),
        cost_estimate=pl.CostEstimate(flops=4_000_000_000, bytes_accessed=2_000_000, transcendentals=0),
        name="convert_base",
    )(slot, trajectory, order)


def vectors_kernel(vec_ref, order_ref, core_ref, head_ref, tail_ref):
    y = split_dot(vec_ref[0, 0].reshape(LEV * LON, NLAT), order_ref[...])
    scatter_rows(y, core_ref.at[0, 0])
    pack_edges(core_ref.at[0, 0], head_ref, tail_ref, (0, 0))


def convert_vectors(vectors, order):
    nv = vectors.shape[0]
    return pl.pallas_call(
        vectors_kernel,
        grid=(nv, 3),
        in_specs=[
            pl.BlockSpec((1, 1, LEV, LON, NLAT), lambda v, c: (v, c, 0, 0, 0)),
            pl.BlockSpec((NLAT, NLAT), lambda v, c: (0, 0)),
        ],
        out_specs=[
            pl.BlockSpec((1, 1, NK, CORE, LANES), lambda v, c: (v, c, 0, 0, 0)),
            pl.BlockSpec((1, 1, NK, RIM + NEAR, LANES), lambda v, c: (v, c, 0, 0, 0)),
            pl.BlockSpec((1, 1, NK, RIM + NEAR, LANES), lambda v, c: (v, c, 0, 0, 0)),
        ],
        out_shape=[
            jax.ShapeDtypeStruct((nv, 3, NK, CORE, LANES), F32),
            jax.ShapeDtypeStruct((nv, 3, NK, RIM + NEAR, LANES), BF16),
            jax.ShapeDtypeStruct((nv, 3, NK, RIM + NEAR, LANES), BF16),
        ],
        compiler_params=pltpu.CompilerParams(vmem_limit_bytes=VMEM_LIMIT),
        cost_estimate=pl.CostEstimate(flops=4_000_000_000, bytes_accessed=7_000_000, transcendentals=0),
        name="convert_vectors",
    )(vectors, order)


def lat_difference(v, masks):
    first, last = masks
    below = jnp.where(first, 0.0, pltpu.roll(v[3], 1, axis=1))
    above = jnp.where(last, 0.0, pltpu.roll(v[0], LANES - 1, axis=1))
    return [v[1] - below, v[2] - v[0], v[3] - v[1], above - v[2]]


def lane_masks():
    lane = lax.broadcasted_iota(jnp.int32, (8, LANES), 1)
    return lane == 0, lane == LANES - 1


def derive(base, der, row, count):
    masks = lane_masks()
    for c in range(3):
        win = [[base[c, k, pl.ds(row + 8 * i - 16, 8), :] for k in range(NK)] for i in range(count + 4)]
        for i in range(count):
            at = pl.ds(row + 8 * i, 8)
            diff = lat_difference(win[i + 2], masks)
            for k in range(NK):
                dx = (8.0 * (win[i + 3][k] - win[i + 1][k]) - (win[i + 4][k] - win[i][k])) * (-COURANT / 12.0)
                dy = diff[k] * (-COURANT / 2.0)
                der[2 + c, k, at, :] = dx + 1.0 if c == 0 else dx
                der[5 + c, k, at, :] = dy + 1.0 if c == 1 else dy
                if c == 0:
                    der[0, k, at, :] = win[i + 2][k] * (-COURANT / 12.0)
                if c == 1:
                    der[1, k, at, :] = win[i + 2][k] * (-COURANT / 2.0)


def stage(src, start, der, row, count, keep, scale, put):
    masks = lane_masks()
    mid = [[[src[c, k, pl.ds(row + 8 * i, 8), :] for k in range(NK)] for i in range(count)] for c in range(2)]
    for c in range(3):
        win = [[src[c, k, pl.ds(row + 8 * i - 16, 8), :] for k in range(NK)] for i in range(count + 4)]
        for i in range(count):
            at = pl.ds(row + 8 * i, 8)
            diff = lat_difference(win[i + 2], masks)
            for k in range(NK):
                dx = 8.0 * (win[i + 3][k] - win[i + 1][k]) - (win[i + 4][k] - win[i][k])
                s = der[0, k, at, :] * dx + der[1, k, at, :] * diff[k]
                s = s + mid[0][i][k] * der[2 + c, k, at, :] + mid[1][i][k] * der[5 + c, k, at, :]
                if c == 2:
                    s = s + win[i + 2][k]
                if keep:
                    s = s + keep * start[c, k, at, :]
                if scale != 1.0:
                    s = s * scale
                put(c, k, row + 8 * i, s)


def sweep(low, high, count, body):
    rows = count * LEV

    def at(i, carry):
        body(pl.multiple_of(low + i * rows, LEV))
        return carry

    lax.fori_loop(0, (high - low) // rows, at, 0)


def step_kernel(choices, last, *refs):
    which_ref, p_ref, left_ref, right_ref = refs[:4]
    sets = [refs[4 + 3 * i : 7 + 3 * i] for i in range(len(choices))]
    rest = refs[4 + 3 * len(choices) :]
    if last:
        order_ref, out_ref, fetched, base, der, one, two, three, sems = rest
    else:
        out_ref, head_ref, tail_ref, fetched, base, der, one, two, three, sems = rest

    def copies(group):
        core, left, right = group
        return [
            pltpu.make_async_copy(left, fetched.at[:, :, pl.ds(0, RIM), :], sems.at[0]),
            pltpu.make_async_copy(core, fetched.at[:, :, pl.ds(RIM, CORE), :], sems.at[1]),
            pltpu.make_async_copy(right, fetched.at[:, :, pl.ds(RIM + CORE, RIM), :], sems.at[2]),
        ]

    v = pl.program_id(0)

    @pl.when(v == 0)
    def _():
        for choice, group in zip(choices, sets):

            @pl.when(which_ref[0] == choice)
            def _(group=group):
                for copy in copies(group):
                    copy.start()
                for copy in copies(group):
                    copy.wait()

        for c in range(3):
            for k in range(NK):
                base[c, k] = fetched[c, k].astype(F32)
        sweep(2 * LEV, EXT - 2 * LEV, 2, lambda row: derive(base, der, row, 2))

    for c in range(3):
        for k in range(NK):
            one[c, k, pl.ds(RIM, CORE), :] = p_ref[0, c, k]
            far = left_ref[0, c, k, pl.ds(0, RIM), :].astype(F32)
            near = left_ref[0, c, k, pl.ds(RIM, NEAR), :].astype(F32)
            one[c, k, pl.ds(0, RIM - NEAR), :] = far[: RIM - NEAR]
            one[c, k, pl.ds(RIM - NEAR, NEAR), :] = far[RIM - NEAR :] + near
            far = right_ref[0, c, k, pl.ds(0, RIM), :].astype(F32)
            near = right_ref[0, c, k, pl.ds(RIM, NEAR), :].astype(F32)
            one[c, k, pl.ds(RIM + CORE, NEAR), :] = far[:NEAR] + near
            one[c, k, pl.ds(RIM + CORE + NEAR, RIM - NEAR), :] = far[NEAR:]

    def into(ref, shift=0):
        def put(c, k, row, s):
            ref[c, k, pl.ds(row - shift, LEV), :] = s

        return put

    final = three if last else out_ref.at[0]
    sweep(2 * LEV, EXT - 2 * LEV, 2, lambda row: stage(one, one, der, row, 2, 0.0, 1.0, into(two)))
    sweep(4 * LEV, EXT - 4 * LEV, 2, lambda row: stage(two, one, der, row, 2, 3.0, 1.0, into(three)))
    if last:
        final = two
    sweep(
        6 * LEV,
        EXT - 6 * LEV,
        2,
        lambda row: stage(three, one, der, row, 2, 2.0, 1.0 / 6.0, into(final, RIM)),
    )
    if last:
        for c in range(3):
            out_ref[0, c] = split_dot(gather_rows(two.at[c]), order_ref[...]).reshape(LEV, LON, NLAT)
    else:
        for c in range(3):
            pack_edges(out_ref.at[0, c], head_ref, tail_ref, (0, c))


def advance(which, pert, edges, choices, groups, order, last):
    nv = pert.shape[0]
    anywhere = pl.BlockSpec(memory_space=pl.ANY)
    edge = pl.BlockSpec((1, 3, NK, RIM + NEAR, LANES), lambda v: (v, 0, 0, 0, 0))
    field = pl.BlockSpec((1, 3, NK, CORE, LANES), lambda v: (v, 0, 0, 0, 0))
    in_specs = [pl.BlockSpec(memory_space=pltpu.SMEM), field, edge, edge] + [anywhere] * (3 * len(groups))
    args = [which, pert, *edges] + [part for group in groups for part in group]
    if last:
        in_specs.append(pl.BlockSpec((NLAT, NLAT), lambda v: (0, 0)))
        args.append(order)
        out_specs = pl.BlockSpec((1, 3, LEV, LON, NLAT), lambda v: (v, 0, 0, 0, 0))
        out_shape = jax.ShapeDtypeStruct((nv, 3, LEV, LON, NLAT), F32)
    else:
        out_specs = [field, edge, edge]
        out_shape = [
            jax.ShapeDtypeStruct((nv, 3, NK, CORE, LANES), F32),
            jax.ShapeDtypeStruct((nv, 3, NK, RIM + NEAR, LANES), BF16),
            jax.ShapeDtypeStruct((nv, 3, NK, RIM + NEAR, LANES), BF16),
        ]
    return pl.pallas_call(
        functools.partial(step_kernel, choices, last),
        grid=(nv,),
        in_specs=in_specs,
        out_specs=out_specs,
        out_shape=out_shape,
        scratch_shapes=[
            pltpu.VMEM((3, NK, EXT, LANES), BF16),
            pltpu.VMEM((3, NK, EXT, LANES), F32),
            pltpu.VMEM((8, NK, EXT, LANES), F32),
        ]
        + [pltpu.VMEM((3, NK, EXT, LANES), F32)] * 3
        + [pltpu.SemaphoreType.DMA((3,))],
        compiler_params=pltpu.CompilerParams(vmem_limit_bytes=VMEM_LIMIT),
        cost_estimate=pl.CostEstimate(flops=9_000_000_000, bytes_accessed=9_000_000, transcendentals=0),
        name="last_step" if last else "step",
    )(*args)


def neighbours(head, tail):
    count = lax.axis_size("tile")
    left = lax.ppermute(tail, "tile", [(i, (i + 1) % count) for i in range(count)])
    right = lax.ppermute(head, "tile", [((i + 1) % count, i) for i in range(count)])
    return left, right


def on_device(order, order_back, vectors, trajectory, slot_table):
    slots = trajectory.shape[0]
    me = lax.axis_index("member")
    owner = slot_table // slots
    local = slot_table % slots
    mine = owner == me
    first = jnp.where(mine[0], local[0], jnp.where(mine[1], local[1], local[2]))
    ranks = [sum((owner[e] == owner[s]).astype(jnp.int32) for e in range(s)) if s else jnp.int32(0) for s in range(STEPS)]
    which = [jnp.where(mine[s], ranks[s], 2 + ranks[s]).reshape(1) for s in range(STEPS)]

    swap = [(0, 1), (1, 0)]
    own, got = [], []
    for turn in range(2):
        slot = jnp.where(turn == 0, first, 1 - first).reshape(1)
        core, head, tail = convert_base(slot, trajectory, order)
        got.append(lax.ppermute(core, "member", swap))
        own.append((core, head, tail))
    own = [(core, *neighbours(head, tail)) for core, head, tail in own]
    got = [(core, *neighbours(core[:, :, :RIM], core[:, :, CORE - RIM :])) for core in got]
    groups = {0: own[0], 1: own[1], 2: got[0], 3: got[1]}

    pert, head, tail = convert_vectors(vectors, order)
    for s in range(STEPS):
        edges = neighbours(head, tail)
        choices = (0, 2) if s == 0 else (1, 3) if s == STEPS - 1 else (0, 1, 2, 3)
        last = s == STEPS - 1
        done = advance(which[s], pert, edges, choices, [groups[i] for i in choices], order_back, last)
        if last:
            return done
        pert, head, tail = done


def solution(mesh):
    order = lane_order()

    def program(vectors, trajectory, slot_table):
        body = functools.partial(on_device, jnp.asarray(order, BF16), jnp.asarray(order.T, BF16))
        spec = P("member", None, None, "tile", None)
        return jax.shard_map(body, mesh=mesh, in_specs=(spec, spec, P()), out_specs=spec, check_vma=False)(
            vectors, trajectory, slot_table
        )

    return program
```

```python
import functools

import jax
import jax.numpy as jnp
import numpy as np
from jax import lax
from jax.experimental import pallas as pl
from jax.experimental.pallas import tpu as pltpu
from jax.sharding import PartitionSpec as P

STEPS = 4
COURANT = 0.8
NK, LANES, LEV, LON, NLAT = 4, 128, 8, 32, 512
CORE = LON * LEV
WIDE = 6
RIM = WIDE * LEV
NEAR = 2 * LEV
EXT = CORE + 2 * RIM
RUN = (8, 4, 4, 4)
VMEM_LIMIT = 34 * 1024 * 1024
F32, BF16 = jnp.float32, jnp.bfloat16


def lane_order():
    order = np.zeros((NLAT, NLAT), np.float32)
    for lat in range(NLAT):
        order[lat, (lat % NK) * LANES + lat // NK] = 1.0
    return order


def dot(a, b):
    return jnp.dot(a, b, preferred_element_type=F32)


def split_dot(x, order):
    high = x.astype(BF16)
    rest = (x - high.astype(F32)).astype(BF16)
    return dot(high, order) + dot(rest, order)


def scatter_rows(y, dst):
    for lev in range(LEV):
        for tile in range(LON // 8):
            for k in range(NK):
                dst[k, pl.ds(tile * 64 + lev, 8, stride=LEV), :] = y[
                    lev * LON + tile * 8 : lev * LON + tile * 8 + 8, k * LANES : (k + 1) * LANES
                ]


def gather_rows(src):
    rows = []
    for lev in range(LEV):
        for tile in range(LON // 8):
            rows.append(
                jnp.concatenate([src[k, pl.ds(tile * 64 + lev, 8, stride=LEV), :] for k in range(NK)], axis=1)
            )
    return jnp.concatenate(rows, axis=0)


def pack_edges(p, head_ref, tail_ref, at):
    for k in range(NK):
        head = p[k, pl.ds(0, RIM), :]
        tail = p[k, pl.ds(CORE - RIM, RIM), :]
        high, last = head.astype(BF16), tail.astype(BF16)
        head_ref[(*at, k, pl.ds(0, RIM), slice(None))] = high
        head_ref[(*at, k, pl.ds(RIM, NEAR), slice(None))] = (head[:NEAR] - high[:NEAR].astype(F32)).astype(BF16)
        tail_ref[(*at, k, pl.ds(0, RIM), slice(None))] = last
        tail_ref[(*at, k, pl.ds(RIM, NEAR), slice(None))] = (tail[RIM - NEAR :] - last[RIM - NEAR :].astype(F32)).astype(BF16)


def timetable(table_ref, slots):
    me = lax.axis_index("member")
    owner = [lax.div(table_ref[s], slots) for s in range(STEPS)]
    local = [lax.rem(table_ref[s], slots) for s in range(STEPS)]
    first = jnp.where(owner[0] == me, local[0], jnp.where(owner[1] == me, local[1], local[2]))
    which = []
    for s in range(STEPS):
        rank = jnp.int32(0)
        for e in range(s):
            rank = rank + jnp.where(owner[e] == owner[s], 1, 0)
        which.append(jnp.where(owner[s] == me, rank, 2 + rank))
    return (first, 1 - first), which


def base_kernel(table_ref, traj_ref, order_ref, core_a, core_b, head_ref, tail_ref, rows):
    turns, _ = timetable(table_ref, traj_ref.shape[0])
    for turn, core_ref in enumerate((core_a, core_b)):
        for c in range(3):
            scatter_rows(dot(traj_ref[turns[turn], c].reshape(LEV * LON, NLAT), order_ref[...]), rows.at[c])
            for k in range(NK):
                core_ref[c, k] = rows[c, k].astype(BF16)
                head_ref[turn, c, k] = rows[c, k, pl.ds(0, RIM), :].astype(BF16)
                tail_ref[turn, c, k] = rows[c, k, pl.ds(CORE - RIM, RIM), :].astype(BF16)


def convert_base(table, trajectory, order):
    return pl.pallas_call(
        base_kernel,
        in_specs=[pl.BlockSpec(memory_space=pltpu.SMEM)] + [pl.BlockSpec(memory_space=pltpu.VMEM)] * 2,
        out_specs=[pl.BlockSpec(memory_space=pltpu.VMEM)] * 4,
        out_shape=[jax.ShapeDtypeStruct((3, NK, CORE, LANES), BF16)] * 2
        + [jax.ShapeDtypeStruct((2, 3, NK, RIM, LANES), BF16)] * 2,
        scratch_shapes=[pltpu.VMEM((3, NK, CORE, LANES), F32)],
        compiler_params=pltpu.CompilerParams(vmem_limit_bytes=VMEM_LIMIT),
        cost_estimate=pl.CostEstimate(flops=1_000_000, bytes_accessed=100_000, transcendentals=0),
        name="convert_base",
    )(table, trajectory, order)


def vectors_kernel(vec_ref, order_ref, core_ref, head_ref, tail_ref):
    y = split_dot(vec_ref[0, 0].reshape(LEV * LON, NLAT), order_ref[...])
    scatter_rows(y, core_ref.at[0, 0])
    pack_edges(core_ref.at[0, 0], head_ref, tail_ref, (0, 0))


def convert_vectors(vectors, order):
    nv = vectors.shape[0]
    return pl.pallas_call(
        vectors_kernel,
        grid=(nv, 3),
        in_specs=[
            pl.BlockSpec((1, 1, LEV, LON, NLAT), lambda v, c: (v, c, 0, 0, 0)),
            pl.BlockSpec((NLAT, NLAT), lambda v, c: (0, 0)),
        ],
        out_specs=[
            pl.BlockSpec((1, 1, NK, CORE, LANES), lambda v, c: (v, c, 0, 0, 0)),
            pl.BlockSpec((1, 1, NK, RIM + NEAR, LANES), lambda v, c: (v, c, 0, 0, 0)),
            pl.BlockSpec((1, 1, NK, RIM + NEAR, LANES), lambda v, c: (v, c, 0, 0, 0)),
        ],
        out_shape=[
            jax.ShapeDtypeStruct((nv, 3, NK, CORE, LANES), F32),
            jax.ShapeDtypeStruct((nv, 3, NK, RIM + NEAR, LANES), BF16),
            jax.ShapeDtypeStruct((nv, 3, NK, RIM + NEAR, LANES), BF16),
        ],
        compiler_params=pltpu.CompilerParams(vmem_limit_bytes=VMEM_LIMIT),
        cost_estimate=pl.CostEstimate(flops=1_000_000, bytes_accessed=100_000, transcendentals=0),
        name="convert_vectors",
    )(vectors, order)


def lat_difference(v, masks):
    first, last = masks
    below = jnp.where(first, 0.0, pltpu.roll(v[3], 1, axis=1))
    above = jnp.where(last, 0.0, pltpu.roll(v[0], LANES - 1, axis=1))
    return [v[1] - below, v[2] - v[0], v[3] - v[1], above - v[2]]


def lane_masks():
    lane = lax.broadcasted_iota(jnp.int32, (8, LANES), 1)
    return lane == 0, lane == LANES - 1


def derive(base, der, row, count):
    masks = lane_masks()
    for c in range(3):
        win = [[base[c, k, pl.ds(row + 8 * i - 16, 8), :] for k in range(NK)] for i in range(count + 4)]
        for i in range(count):
            at = pl.ds(row + 8 * i, 8)
            diff = lat_difference(win[i + 2], masks)
            for k in range(NK):
                dx = (8.0 * (win[i + 3][k] - win[i + 1][k]) - (win[i + 4][k] - win[i][k])) * (-COURANT / 12.0)
                dy = diff[k] * (-COURANT / 2.0)
                der[2 + c, k, at, :] = dx + 1.0 if c == 0 else dx
                der[5 + c, k, at, :] = dy + 1.0 if c == 1 else dy
                if c == 0:
                    der[0, k, at, :] = win[i + 2][k] * (-COURANT / 12.0)
                if c == 1:
                    der[1, k, at, :] = win[i + 2][k] * (-COURANT / 2.0)


def stage(src, start, der, row, count, keep, scale, put):
    masks = lane_masks()
    mid = [[[src[c, k, pl.ds(row + 8 * i, 8), :] for k in range(NK)] for i in range(count)] for c in range(2)]
    for c in range(3):
        win = [[src[c, k, pl.ds(row + 8 * i - 16, 8), :] for k in range(NK)] for i in range(count + 4)]
        for i in range(count):
            at = pl.ds(row + 8 * i, 8)
            diff = lat_difference(win[i + 2], masks)
            for k in range(NK):
                dx = 8.0 * (win[i + 3][k] - win[i + 1][k]) - (win[i + 4][k] - win[i][k])
                s = der[0, k, at, :] * dx + der[1, k, at, :] * diff[k]
                s = s + mid[0][i][k] * der[2 + c, k, at, :] + mid[1][i][k] * der[5 + c, k, at, :]
                if c == 2:
                    s = s + win[i + 2][k]
                if keep:
                    s = s + keep * start[c, k, at, :]
                if scale != 1.0:
                    s = s * scale
                put(c, k, row + 8 * i, s)


def sweep(low, high, count, body):
    rows = count * LEV

    def at(i, carry):
        body(pl.multiple_of(low + i * rows, LEV))
        return carry

    lax.fori_loop(0, (high - low) // rows, at, 0)


def widen_base(core, left, right, base):
    for c in range(3):
        for k in range(NK):
            base[c, k, pl.ds(0, RIM), :] = left[c, k].astype(F32)
            base[c, k, pl.ds(RIM, CORE), :] = core[c, k].astype(F32)
            base[c, k, pl.ds(RIM + CORE, RIM), :] = right[c, k].astype(F32)


def widen_pert(core, left, right, wide):
    for c in range(3):
        for k in range(NK):
            wide[c, k, pl.ds(RIM, CORE), :] = core[c, k]
            far = left[c, k, pl.ds(0, RIM), :].astype(F32)
            near = left[c, k, pl.ds(RIM, NEAR), :].astype(F32)
            wide[c, k, pl.ds(0, RIM - NEAR), :] = far[: RIM - NEAR]
            wide[c, k, pl.ds(RIM - NEAR, NEAR), :] = far[RIM - NEAR :] + near
            far = right[c, k, pl.ds(0, RIM), :].astype(F32)
            near = right[c, k, pl.ds(RIM, NEAR), :].astype(F32)
            wide[c, k, pl.ds(RIM + CORE, NEAR), :] = far[:NEAR] + near
            wide[c, k, pl.ds(RIM + CORE + NEAR, RIM - NEAR), :] = far[NEAR:]


def into(ref, shift=0):
    def put(c, k, row, s):
        ref[c, k, pl.ds(row - shift, LEV), :] = s

    return put


def step_kernel(step, slots, last, *refs):
    table_ref, p_ref, left_ref, right_ref, own_a, own_b, own_left, own_right = refs[:8]
    sets = [(0, own_a, own_left.at[0], own_right.at[0]), (1, own_b, own_left.at[1], own_right.at[1])]
    taken = 8
    for choice in (2, 3) if step else (2,):
        sets.append((choice, *refs[taken : taken + 3]))
        taken += 3
    rest = refs[taken:]
    if last:
        order_ref, out_ref, base, der, one, two, three = rest
    else:
        out_ref, head_ref, tail_ref, base, der, one, two, three = rest
    _, which = timetable(table_ref, slots)
    for choice, *group in sets:

        @pl.when(which[step] == choice)
        def _(group=group):
            widen_base(*group, base)

    sweep(2 * LEV, EXT - 2 * LEV, RUN[0], lambda row: derive(base, der, row, RUN[0]))

    def vector(v, carry):
        widen_pert(p_ref.at[v], left_ref.at[v], right_ref.at[v], one)
        final = two if last else out_ref.at[v]
        sweep(2 * LEV, EXT - 2 * LEV, RUN[1], lambda row: stage(one, one, der, row, RUN[1], 0.0, 1.0, into(two)))
        sweep(4 * LEV, EXT - 4 * LEV, RUN[2], lambda row: stage(two, one, der, row, RUN[2], 3.0, 1.0, into(three)))
        sweep(
            6 * LEV,
            EXT - 6 * LEV,
            RUN[3],
            lambda row: stage(three, one, der, row, RUN[3], 2.0, 1.0 / 6.0, into(final, RIM)),
        )
        for c in range(3):
            if last:
                out_ref[v, c] = split_dot(gather_rows(two.at[c]), order_ref[...]).reshape(LEV, LON, NLAT)
            else:
                pack_edges(out_ref.at[v, c], head_ref.at[v], tail_ref.at[v], (c,))
        return carry

    lax.fori_loop(0, p_ref.shape[0], vector, 0)


def advance(step, slots, table, pert, edges, bases, order):
    last = step == STEPS - 1
    nv = pert.shape[0]
    args = [table, pert, *edges, *bases]
    if last:
        args.append(order)
        out_shape = jax.ShapeDtypeStruct((nv, 3, LEV, LON, NLAT), F32)
        out_specs = pl.BlockSpec(memory_space=pltpu.VMEM)
    else:
        out_shape = [
            jax.ShapeDtypeStruct((nv, 3, NK, CORE, LANES), F32),
            jax.ShapeDtypeStruct((nv, 3, NK, RIM + NEAR, LANES), BF16),
            jax.ShapeDtypeStruct((nv, 3, NK, RIM + NEAR, LANES), BF16),
        ]
        out_specs = [pl.BlockSpec(memory_space=pltpu.VMEM)] * 3
    return pl.pallas_call(
        functools.partial(step_kernel, step, slots, last),
        in_specs=[pl.BlockSpec(memory_space=pltpu.SMEM)] + [pl.BlockSpec(memory_space=pltpu.VMEM)] * (len(args) - 1),
        out_specs=out_specs,
        out_shape=out_shape,
        scratch_shapes=[pltpu.VMEM((3, NK, EXT, LANES), F32), pltpu.VMEM((8, NK, EXT, LANES), F32)]
        + [pltpu.VMEM((3, NK, EXT, LANES), F32)] * 3,
        compiler_params=pltpu.CompilerParams(vmem_limit_bytes=VMEM_LIMIT),
        cost_estimate=pl.CostEstimate(flops=1_000_000, bytes_accessed=100_000, transcendentals=0),
        name="last_step" if last else "step",
    )(*args)


def neighbours(head, tail):
    count = lax.axis_size("tile")
    left = lax.ppermute(tail, "tile", [(i, (i + 1) % count) for i in range(count)])
    right = lax.ppermute(head, "tile", [((i + 1) % count, i) for i in range(count)])
    return left, right


def on_device(order, order_back, vectors, trajectory, slot_table):
    slots = trajectory.shape[0]
    swap = [(0, 1), (1, 0)]
    own_a, own_b, head, tail = convert_base(slot_table, trajectory, order)
    got = [lax.ppermute(core, "member", swap) for core in (own_a, own_b)]
    own = (own_a, own_b, *neighbours(head, tail))
    got = [(core, *neighbours(core[:, :, :RIM], core[:, :, CORE - RIM :])) for core in got]

    pert, head, tail = convert_vectors(vectors, order)
    for step in range(STEPS):
        edges = neighbours(head, tail)
        bases = (*own, *got[0], *got[1]) if step else (*own, *got[0])
        done = advance(step, slots, slot_table, pert, edges, bases, order_back)
        if step == STEPS - 1:
            return done
        pert, head, tail = done


def solution(mesh):
    order = lane_order()

    def program(vectors, trajectory, slot_table):
        body = functools.partial(on_device, jnp.asarray(order, BF16), jnp.asarray(order.T, BF16))
        spec = P("member", None, None, "tile", None)
        return jax.shard_map(body, mesh=mesh, in_specs=(spec, spec, P()), out_specs=spec, check_vma=False)(
            vectors, trajectory, slot_table
        )

    return program
```

```python
import functools

import jax
import jax.numpy as jnp
import numpy as np
from jax import lax
from jax.experimental import pallas as pl
from jax.experimental.pallas import tpu as pltpu
from jax.sharding import PartitionSpec as P

STEPS = 4
COURANT = 0.8
NK, LANES, LEV, LON, NLAT = 4, 128, 8, 32, 512
CORE = LON * LEV
WIDE = 6
RIM = WIDE * LEV
NEAR = 2 * LEV
RUN = 4
SIDE = 16 * LEV
HANDED = (((2, 8), (26, 4)), ((4, 10), (24, 2)))
INTERIOR_FLOPS = 1_000_000
VMEM_LIMIT = 34 * 1024 * 1024
F32, BF16 = jnp.float32, jnp.bfloat16


def lane_order():
    order = np.zeros((NLAT, NLAT), np.float32)
    for lat in range(NLAT):
        order[lat, (lat % NK) * LANES + lat // NK] = 1.0
    return order


def dot(a, b):
    return jnp.dot(a, b, preferred_element_type=F32)


def split_dot(x, order):
    high = x.astype(BF16)
    rest = (x - high.astype(F32)).astype(BF16)
    return dot(high, order) + dot(rest, order)


def scatter_rows(y, dst):
    for lev in range(LEV):
        for tile in range(LON // 8):
            for k in range(NK):
                dst[k, pl.ds(tile * 64 + lev, 8, stride=LEV), :] = y[
                    lev * LON + tile * 8 : lev * LON + tile * 8 + 8, k * LANES : (k + 1) * LANES
                ]


def gather_rows(src):
    rows = []
    for lev in range(LEV):
        for tile in range(LON // 8):
            rows.append(
                jnp.concatenate([src[k, pl.ds(tile * 64 + lev, 8, stride=LEV), :] for k in range(NK)], axis=1)
            )
    return jnp.concatenate(rows, axis=0)


def pack_edges(p, head_ref, tail_ref, at):
    for k in range(NK):
        head = p[k, pl.ds(0, RIM), :]
        tail = p[k, pl.ds(CORE - RIM, RIM), :]
        high, last = head.astype(BF16), tail.astype(BF16)
        head_ref[(*at, k, pl.ds(0, RIM), slice(None))] = high
        head_ref[(*at, k, pl.ds(RIM, NEAR), slice(None))] = (head[:NEAR] - high[:NEAR].astype(F32)).astype(BF16)
        tail_ref[(*at, k, pl.ds(0, RIM), slice(None))] = last
        tail_ref[(*at, k, pl.ds(RIM, NEAR), slice(None))] = (tail[RIM - NEAR :] - last[RIM - NEAR :].astype(F32)).astype(BF16)


def timetable(table_ref, slots):
    me = lax.axis_index("member")
    owner = [lax.div(table_ref[s], slots) for s in range(STEPS)]
    local = [lax.rem(table_ref[s], slots) for s in range(STEPS)]
    first = jnp.where(owner[0] == me, local[0], jnp.where(owner[1] == me, local[1], local[2]))
    which = []
    for s in range(STEPS):
        rank = jnp.int32(0)
        for e in range(s):
            rank = rank + jnp.where(owner[e] == owner[s], 1, 0)
        which.append(jnp.where(owner[s] == me, rank, 2 + rank))
    return (first, 1 - first), which


def base_kernel(table_ref, traj_ref, order_ref, core_a, core_b, head_ref, tail_ref, rows):
    turns, _ = timetable(table_ref, traj_ref.shape[0])
    for turn, core_ref in enumerate((core_a, core_b)):
        for c in range(3):
            scatter_rows(dot(traj_ref[turns[turn], c].reshape(LEV * LON, NLAT), order_ref[...]), rows.at[c])
            for k in range(NK):
                core_ref[c, k] = rows[c, k].astype(BF16)
                head_ref[turn, c, k] = rows[c, k, pl.ds(0, RIM), :].astype(BF16)
                tail_ref[turn, c, k] = rows[c, k, pl.ds(CORE - RIM, RIM), :].astype(BF16)


def convert_base(table, trajectory, order):
    return pl.pallas_call(
        base_kernel,
        in_specs=[pl.BlockSpec(memory_space=pltpu.SMEM)] + [pl.BlockSpec(memory_space=pltpu.VMEM)] * 2,
        out_specs=[pl.BlockSpec(memory_space=pltpu.VMEM)] * 4,
        out_shape=[jax.ShapeDtypeStruct((3, NK, CORE, LANES), BF16)] * 2
        + [jax.ShapeDtypeStruct((2, 3, NK, RIM, LANES), BF16)] * 2,
        scratch_shapes=[pltpu.VMEM((3, NK, CORE, LANES), F32)],
        compiler_params=pltpu.CompilerParams(vmem_limit_bytes=VMEM_LIMIT),
        cost_estimate=pl.CostEstimate(flops=1_000_000, bytes_accessed=100_000, transcendentals=0),
        name="convert_base",
    )(table, trajectory, order)


def vectors_kernel(vec_ref, order_ref, core_ref, head_ref, tail_ref):
    y = split_dot(vec_ref[0, 0].reshape(LEV * LON, NLAT), order_ref[...])
    scatter_rows(y, core_ref.at[0, 0])
    pack_edges(core_ref.at[0, 0], head_ref, tail_ref, (0, 0))


def convert_vectors(vectors, order):
    nv = vectors.shape[0]
    return pl.pallas_call(
        vectors_kernel,
        grid=(nv, 3),
        in_specs=[
            pl.BlockSpec((1, 1, LEV, LON, NLAT), lambda v, c: (v, c, 0, 0, 0)),
            pl.BlockSpec((NLAT, NLAT), lambda v, c: (0, 0)),
        ],
        out_specs=[
            pl.BlockSpec((1, 1, NK, CORE, LANES), lambda v, c: (v, c, 0, 0, 0)),
            pl.BlockSpec((1, 1, NK, RIM + NEAR, LANES), lambda v, c: (v, c, 0, 0, 0)),
            pl.BlockSpec((1, 1, NK, RIM + NEAR, LANES), lambda v, c: (v, c, 0, 0, 0)),
        ],
        out_shape=[
            jax.ShapeDtypeStruct((nv, 3, NK, CORE, LANES), F32),
            jax.ShapeDtypeStruct((nv, 3, NK, RIM + NEAR, LANES), BF16),
            jax.ShapeDtypeStruct((nv, 3, NK, RIM + NEAR, LANES), BF16),
        ],
        compiler_params=pltpu.CompilerParams(vmem_limit_bytes=VMEM_LIMIT),
        cost_estimate=pl.CostEstimate(flops=1_000_000, bytes_accessed=100_000, transcendentals=0),
        name="convert_vectors",
    )(vectors, order)


def lat_difference(v, masks):
    first, last = masks
    below = jnp.where(first, 0.0, pltpu.roll(v[3], 1, axis=1))
    above = jnp.where(last, 0.0, pltpu.roll(v[0], LANES - 1, axis=1))
    return [v[1] - below, v[2] - v[0], v[3] - v[1], above - v[2]]


def lane_masks():
    lane = lax.broadcasted_iota(jnp.int32, (8, LANES), 1)
    return lane == 0, lane == LANES - 1


def derive(base, der, row, count):
    masks = lane_masks()
    for c in range(3):
        win = [[base[c, k, pl.ds(row + 8 * i - 16, 8), :] for k in range(NK)] for i in range(count + 4)]
        for i in range(count):
            at = pl.ds(row + 8 * i, 8)
            diff = lat_difference(win[i + 2], masks)
            for k in range(NK):
                dx = (8.0 * (win[i + 3][k] - win[i + 1][k]) - (win[i + 4][k] - win[i][k])) * (-COURANT / 12.0)
                dy = diff[k] * (-COURANT / 2.0)
                der[2 + c, k, at, :] = dx + 1.0 if c == 0 else dx
                der[5 + c, k, at, :] = dy + 1.0 if c == 1 else dy
                if c == 0:
                    der[0, k, at, :] = win[i + 2][k] * (-COURANT / 12.0)
                if c == 1:
                    der[1, k, at, :] = win[i + 2][k] * (-COURANT / 2.0)


def stage(src, start, der, row, count, keep, scale, put):
    masks = lane_masks()
    mid = [[[src[c, k, pl.ds(row + 8 * i, 8), :] for k in range(NK)] for i in range(count)] for c in range(2)]
    for c in range(3):
        win = [[src[c, k, pl.ds(row + 8 * i - 16, 8), :] for k in range(NK)] for i in range(count + 4)]
        for i in range(count):
            at = pl.ds(row + 8 * i, 8)
            diff = lat_difference(win[i + 2], masks)
            for k in range(NK):
                dx = 8.0 * (win[i + 3][k] - win[i + 1][k]) - (win[i + 4][k] - win[i][k])
                s = der[0, k, at, :] * dx + der[1, k, at, :] * diff[k]
                s = s + mid[0][i][k] * der[2 + c, k, at, :] + mid[1][i][k] * der[5 + c, k, at, :]
                if c == 2:
                    s = s + win[i + 2][k]
                if keep:
                    s = s + keep * start[c, k, at, :]
                if scale != 1.0:
                    s = s * scale
                put(c, k, row + 8 * i, s)


def sweep(low, high, count, body):
    rows = count * LEV

    def at(i, carry):
        body(pl.multiple_of(low + i * rows, LEV))
        return carry

    lax.fori_loop(0, (high - low) // rows, at, 0)


def choices_of(step):
    return (0, 2) if step == 0 else (0, 1, 2, 3)


def into(ref, shift=0):
    def put(c, k, row, s):
        ref[c, k, pl.ds(row + shift, LEV), :] = s

    return put


def rows_of(low, count):
    return pl.ds(low * LEV, count * LEV)


def interior_kernel(step, slots, table_ref, p_ref, *refs):
    choices = choices_of(step)
    cores = refs[: len(choices)]
    out_ref, handed_ref, base, der, two, three = refs[len(choices) :]
    _, which = timetable(table_ref, slots)
    for choice, core in zip(choices, cores):

        @pl.when(which[step] == choice)
        def _(core=core):
            for c in range(3):
                for k in range(NK):
                    base[c, k] = core[c, k].astype(F32)

    sweep(2 * LEV, 30 * LEV, RUN, lambda row: derive(base, der, row, RUN))

    def vector(v, carry):
        one = p_ref.at[v]
        last = into(out_ref.at[v])
        sweep(2 * LEV, 30 * LEV, RUN, lambda row: stage(one, one, der, row, RUN, 0.0, 1.0, into(two)))
        sweep(4 * LEV, 28 * LEV, RUN, lambda row: stage(two, one, der, row, RUN, 3.0, 1.0, into(three)))
        sweep(6 * LEV, 26 * LEV, RUN, lambda row: stage(three, one, der, row, RUN, 2.0, 1.0 / 6.0, last))
        for c in range(3):
            for k in range(NK):
                for i, (held, places) in enumerate(zip((two, three), HANDED)):
                    for side, (low, _) in enumerate(places):
                        handed_ref[v, c, k, rows_of(8 * i + 4 * side, 4), :] = held[c, k, rows_of(low, 4), :]
        return carry

    lax.fori_loop(0, p_ref.shape[0], vector, 0)


def interior(step, slots, table, pert, cores):
    nv = pert.shape[0]
    args = [table, pert, *cores]
    field = pltpu.VMEM((3, NK, CORE, LANES), F32)
    return pl.pallas_call(
        functools.partial(interior_kernel, step, slots),
        in_specs=[pl.BlockSpec(memory_space=pltpu.SMEM)] + [pl.BlockSpec(memory_space=pltpu.VMEM)] * (len(args) - 1),
        out_specs=[pl.BlockSpec(memory_space=pltpu.VMEM)] * 2,
        out_shape=[
            jax.ShapeDtypeStruct((nv, 3, NK, CORE, LANES), F32),
            jax.ShapeDtypeStruct((nv, 3, NK, 16 * LEV, LANES), F32),
        ],
        scratch_shapes=[field, pltpu.VMEM((8, NK, CORE, LANES), F32), field, field],
        compiler_params=pltpu.CompilerParams(vmem_limit_bytes=VMEM_LIMIT),
        cost_estimate=pl.CostEstimate(flops=INTERIOR_FLOPS, bytes_accessed=100_000, transcendentals=0),
        name="interior",
    )(*args)


def boundary_kernel(step, slots, last, *refs):
    table_ref, p_ref, inner_ref, handed_ref, left_ref, right_ref, own_a, own_b, own_left, own_right = refs[:10]
    sets = [(0, own_a, own_left.at[0], own_right.at[0]), (1, own_b, own_left.at[1], own_right.at[1])]
    taken = 10
    for choice in (2, 3) if step else (2,):
        sets.append((choice, *refs[taken : taken + 3]))
        taken += 3
    rest = refs[taken:]
    if last:
        order_ref, out_ref, base, der, one, two, three, whole = rest
    else:
        out_ref, head_ref, tail_ref, base, der, one, two, three = rest
    _, which = timetable(table_ref, slots)
    for choice, core, left, right in sets:

        @pl.when(which[step] == choice)
        def _(core=core, left=left, right=right):
            for c in range(3):
                for k in range(NK):
                    base[0, c, k, rows_of(0, 6), :] = left[c, k].astype(F32)
                    base[0, c, k, rows_of(6, 10), :] = core[c, k, rows_of(0, 10), :].astype(F32)
                    base[1, c, k, rows_of(0, 10), :] = core[c, k, rows_of(22, 10), :].astype(F32)
                    base[1, c, k, rows_of(10, 6), :] = right[c, k].astype(F32)

    for side, low in enumerate((2, 4)):
        sweep(low * LEV, (low + 10) * LEV, 10, lambda row, side=side: derive(base.at[side], der.at[side], row, 10))

    def vector(v, carry):
        for c in range(3):
            for k in range(NK):
                one[0, c, k, rows_of(6, 10), :] = p_ref[v, c, k, rows_of(0, 10), :]
                high = left_ref[v, c, k, pl.ds(0, RIM), :].astype(F32)
                rest = left_ref[v, c, k, pl.ds(RIM, NEAR), :].astype(F32)
                one[0, c, k, pl.ds(0, RIM - NEAR), :] = high[: RIM - NEAR]
                one[0, c, k, pl.ds(RIM - NEAR, NEAR), :] = high[RIM - NEAR :] + rest
                one[1, c, k, rows_of(0, 10), :] = p_ref[v, c, k, rows_of(22, 10), :]
                high = right_ref[v, c, k, pl.ds(0, RIM), :].astype(F32)
                rest = right_ref[v, c, k, pl.ds(RIM, NEAR), :].astype(F32)
                one[1, c, k, pl.ds(10 * LEV, NEAR), :] = high[:NEAR] + rest
                one[1, c, k, pl.ds(10 * LEV + NEAR, RIM - NEAR), :] = high[NEAR:]
                for i, (held, places) in enumerate(zip((two, three), HANDED)):
                    for side, (_, low) in enumerate(places):
                        held[side, c, k, rows_of(low, 4), :] = handed_ref[v, c, k, rows_of(8 * i + 4 * side, 4), :]
        final = whole if last else out_ref.at[v]
        for side, low in enumerate((2, 8)):
            stage(one.at[side], one.at[side], der.at[side], low * LEV, 6, 0.0, 1.0, into(two.at[side]))
        for side, low in enumerate((4, 6)):
            stage(two.at[side], one.at[side], der.at[side], low * LEV, 6, 3.0, 1.0, into(three.at[side]))
        for side, (low, shift) in enumerate(((6, -6), (4, 22))):
            put = into(final, shift * LEV)
            stage(three.at[side], one.at[side], der.at[side], low * LEV, 6, 2.0, 1.0 / 6.0, put)
        for c in range(3):
            for k in range(NK):
                final[c, k, rows_of(6, 20), :] = inner_ref[v, c, k, rows_of(6, 20), :]
            if last:
                out_ref[v, c] = split_dot(gather_rows(whole.at[c]), order_ref[...]).reshape(LEV, LON, NLAT)
            else:
                pack_edges(out_ref.at[v, c], head_ref.at[v], tail_ref.at[v], (c,))
        return carry

    lax.fori_loop(0, p_ref.shape[0], vector, 0)


def boundary(step, slots, table, pert, inner, edges, bases, order):
    last = step == STEPS - 1
    nv = pert.shape[0]
    args = [table, pert, *inner, *edges, *bases]
    side = pltpu.VMEM((2, 3, NK, SIDE, LANES), F32)
    scratch = [side, pltpu.VMEM((2, 8, NK, SIDE, LANES), F32), side, side, side]
    if last:
        args.append(order)
        scratch.append(pltpu.VMEM((3, NK, CORE, LANES), F32))
        out_shape = jax.ShapeDtypeStruct((nv, 3, LEV, LON, NLAT), F32)
        out_specs = pl.BlockSpec(memory_space=pltpu.VMEM)
    else:
        out_shape = [
            jax.ShapeDtypeStruct((nv, 3, NK, CORE, LANES), F32),
            jax.ShapeDtypeStruct((nv, 3, NK, RIM + NEAR, LANES), BF16),
            jax.ShapeDtypeStruct((nv, 3, NK, RIM + NEAR, LANES), BF16),
        ]
        out_specs = [pl.BlockSpec(memory_space=pltpu.VMEM)] * 3
    return pl.pallas_call(
        functools.partial(boundary_kernel, step, slots, last),
        in_specs=[pl.BlockSpec(memory_space=pltpu.SMEM)] + [pl.BlockSpec(memory_space=pltpu.VMEM)] * (len(args) - 1),
        out_specs=out_specs,
        out_shape=out_shape,
        scratch_shapes=scratch,
        compiler_params=pltpu.CompilerParams(vmem_limit_bytes=VMEM_LIMIT),
        cost_estimate=pl.CostEstimate(flops=1_000_000, bytes_accessed=100_000, transcendentals=0),
        name="last_boundary" if last else "boundary",
    )(*args)


def neighbours(head, tail):
    count = lax.axis_size("tile")
    left = lax.ppermute(tail, "tile", [(i, (i + 1) % count) for i in range(count)])
    right = lax.ppermute(head, "tile", [((i + 1) % count, i) for i in range(count)])
    return left, right


def on_device(order, order_back, vectors, trajectory, slot_table):
    slots = trajectory.shape[0]
    swap = [(0, 1), (1, 0)]
    own_a, own_b, head, tail = convert_base(slot_table, trajectory, order)
    got = [lax.ppermute(core, "member", swap) for core in (own_a, own_b)]
    own = (own_a, own_b, *neighbours(head, tail))

    def with_halo(core):
        return core, *neighbours(core[:, :, :RIM], core[:, :, CORE - RIM :])

    got[0] = with_halo(got[0])
    pert, head, tail = convert_vectors(vectors, order)
    for step in range(STEPS):
        edges = neighbours(head, tail)
        cores = (own_a, own_b, got[0][0], got[1][0] if step else None)
        inner = interior(step, slots, slot_table, pert, [cores[i] for i in choices_of(step)])
        bases = (*own, *got[0], *got[1]) if step else (*own, *got[0])
        done = boundary(step, slots, slot_table, pert, inner, edges, bases, order_back)
        if step == STEPS - 1:
            return done
        pert, head, tail = done
        if step == 0:
            pert, second = lax.optimization_barrier((pert, got[1]))
            got[1] = with_halo(second)


def solution(mesh):
    order = lane_order()

    def program(vectors, trajectory, slot_table):
        body = functools.partial(on_device, jnp.asarray(order, BF16), jnp.asarray(order.T, BF16))
        spec = P("member", None, None, "tile", None)
        return jax.shard_map(body, mesh=mesh, in_specs=(spec, spec, P()), out_specs=spec, check_vma=False)(
            vectors, trajectory, slot_table
        )

    return program
```

```python
import functools

import jax
import jax.numpy as jnp
import numpy as np
from jax import lax
from jax.experimental import pallas as pl
from jax.experimental.pallas import tpu as pltpu
from jax.sharding import PartitionSpec as P

STEPS = 4
COURANT = 0.8
NK, LANES, LEV, LON, NLAT = 4, 128, 8, 32, 512
CORE = LON * LEV
WIDE = 6
RIM = WIDE * LEV
NEAR = 2 * LEV
RUN = (7, 14, 12, 10)
SIDE = 16 * LEV
HANDED = (((2, 8), (26, 4)), ((4, 10), (24, 2)))
INTERIOR_FLOPS = 1_000_000
VMEM_LIMIT = 34 * 1024 * 1024
BASE_VMEM_LIMIT = 61 * 1024 * 1024
F32, BF16 = jnp.float32, jnp.bfloat16


def lane_order():
    order = np.zeros((NLAT, NLAT), np.float32)
    for lat in range(NLAT):
        order[lat, (lat % NK) * LANES + lat // NK] = 1.0
    return order


def dot(a, b):
    return jnp.dot(a, b, preferred_element_type=F32)


def split_dot(x, order):
    high = x.astype(BF16)
    rest = (x - high.astype(F32)).astype(BF16)
    return dot(high, order) + dot(rest, order)


def scatter_rows(y, dst):
    for lev in range(LEV):
        for tile in range(LON // 8):
            for k in range(NK):
                dst[k, pl.ds(tile * 64 + lev, 8, stride=LEV), :] = y[
                    lev * LON + tile * 8 : lev * LON + tile * 8 + 8, k * LANES : (k + 1) * LANES
                ]


def gather_rows(src):
    rows = []
    for lev in range(LEV):
        for tile in range(LON // 8):
            rows.append(
                jnp.concatenate([src[k, pl.ds(tile * 64 + lev, 8, stride=LEV), :] for k in range(NK)], axis=1)
            )
    return jnp.concatenate(rows, axis=0)


def pack_edges(p, head_ref, tail_ref, at):
    for k in range(NK):
        head = p[k, pl.ds(0, RIM), :]
        tail = p[k, pl.ds(CORE - RIM, RIM), :]
        high, last = head.astype(BF16), tail.astype(BF16)
        head_ref[(*at, k, pl.ds(0, RIM), slice(None))] = high
        head_ref[(*at, k, pl.ds(RIM, NEAR), slice(None))] = (head[:NEAR] - high[:NEAR].astype(F32)).astype(BF16)
        tail_ref[(*at, k, pl.ds(0, RIM), slice(None))] = last
        tail_ref[(*at, k, pl.ds(RIM, NEAR), slice(None))] = (tail[RIM - NEAR :] - last[RIM - NEAR :].astype(F32)).astype(BF16)


def timetable(table_ref, slots):
    me = lax.axis_index("member")
    owner = [lax.div(table_ref[s], slots) for s in range(STEPS)]
    local = [lax.rem(table_ref[s], slots) for s in range(STEPS)]
    first = jnp.where(owner[0] == me, local[0], jnp.where(owner[1] == me, local[1], local[2]))
    which = []
    for s in range(STEPS):
        rank = jnp.int32(0)
        for e in range(s):
            rank = rank + jnp.where(owner[e] == owner[s], 1, 0)
        which.append(jnp.where(owner[s] == me, rank, 2 + rank))
    return (first, 1 - first), which


def base_kernel(table_ref, traj_ref, core_a, core_b, head_ref, tail_ref, slots, order_ref, rows, sems):
    turns, _ = timetable(table_ref, traj_ref.shape[0])
    copies = [
        pltpu.make_async_copy(traj_ref.at[turns[turn]], slots.at[turn], sems.at[turn]) for turn in range(2)
    ]
    for copy in copies:
        copy.start()
    lat = lax.broadcasted_iota(jnp.int32, (NLAT, NLAT), 0)
    place = lax.broadcasted_iota(jnp.int32, (NLAT, NLAT), 1)
    order_ref[...] = jnp.where((lat & (NK - 1)) * LANES + (lat >> 2) == place, 1.0, 0.0).astype(BF16)
    for turn, core_ref in enumerate((core_a, core_b)):
        copies[turn].wait()
        for c in range(3):
            scatter_rows(dot(slots[turn, c].reshape(LEV * LON, NLAT), order_ref[...]), rows.at[c])
            for k in range(NK):
                core_ref[c, k] = rows[c, k].astype(BF16)
                head_ref[turn, c, k] = rows[c, k, pl.ds(0, RIM), :].astype(BF16)
                tail_ref[turn, c, k] = rows[c, k, pl.ds(CORE - RIM, RIM), :].astype(BF16)


def convert_base(table, trajectory):
    return pl.pallas_call(
        base_kernel,
        in_specs=[pl.BlockSpec(memory_space=pltpu.SMEM), pl.BlockSpec(memory_space=pl.ANY)],
        out_specs=[pl.BlockSpec(memory_space=pltpu.VMEM)] * 4,
        out_shape=[jax.ShapeDtypeStruct((3, NK, CORE, LANES), BF16)] * 2
        + [jax.ShapeDtypeStruct((2, 3, NK, RIM, LANES), BF16)] * 2,
        scratch_shapes=[
            pltpu.VMEM((2, 3, LEV, LON, NLAT), BF16),
            pltpu.VMEM((NLAT, NLAT), BF16),
            pltpu.VMEM((3, NK, CORE, LANES), F32),
            pltpu.SemaphoreType.DMA((2,)),
        ],
        compiler_params=pltpu.CompilerParams(vmem_limit_bytes=BASE_VMEM_LIMIT),
        cost_estimate=pl.CostEstimate(flops=1_000_000, bytes_accessed=100_000, transcendentals=0),
        name="convert_base",
    )(table, trajectory)


def vectors_kernel(vec_ref, order_ref, core_ref, head_ref, tail_ref):
    y = split_dot(vec_ref[0, 0].reshape(LEV * LON, NLAT), order_ref[...])
    scatter_rows(y, core_ref.at[0, 0])
    pack_edges(core_ref.at[0, 0], head_ref, tail_ref, (0, 0))


def convert_vectors(vectors, order):
    nv = vectors.shape[0]
    return pl.pallas_call(
        vectors_kernel,
        grid=(nv, 3),
        in_specs=[
            pl.BlockSpec((1, 1, LEV, LON, NLAT), lambda v, c: (v, c, 0, 0, 0)),
            pl.BlockSpec((NLAT, NLAT), lambda v, c: (0, 0)),
        ],
        out_specs=[
            pl.BlockSpec((1, 1, NK, CORE, LANES), lambda v, c: (v, c, 0, 0, 0)),
            pl.BlockSpec((1, 1, NK, RIM + NEAR, LANES), lambda v, c: (v, c, 0, 0, 0)),
            pl.BlockSpec((1, 1, NK, RIM + NEAR, LANES), lambda v, c: (v, c, 0, 0, 0)),
        ],
        out_shape=[
            jax.ShapeDtypeStruct((nv, 3, NK, CORE, LANES), F32),
            jax.ShapeDtypeStruct((nv, 3, NK, RIM + NEAR, LANES), BF16),
            jax.ShapeDtypeStruct((nv, 3, NK, RIM + NEAR, LANES), BF16),
        ],
        compiler_params=pltpu.CompilerParams(vmem_limit_bytes=VMEM_LIMIT),
        cost_estimate=pl.CostEstimate(flops=1_000_000, bytes_accessed=100_000, transcendentals=0),
        name="convert_vectors",
    )(vectors, order)


def lat_difference(v, masks):
    first, last = masks
    below = jnp.where(first, 0.0, pltpu.roll(v[3], 1, axis=1))
    above = jnp.where(last, 0.0, pltpu.roll(v[0], LANES - 1, axis=1))
    return [v[1] - below, v[2] - v[0], v[3] - v[1], above - v[2]]


def lane_masks():
    lane = lax.broadcasted_iota(jnp.int32, (8, LANES), 1)
    return lane == 0, lane == LANES - 1


def derive(base, der, row, count):
    masks = lane_masks()
    for c in range(3):
        win = [[base[c, k, pl.ds(row + 8 * i - 16, 8), :] for k in range(NK)] for i in range(count + 4)]
        for i in range(count):
            at = pl.ds(row + 8 * i, 8)
            diff = lat_difference(win[i + 2], masks)
            for k in range(NK):
                dx = (8.0 * (win[i + 3][k] - win[i + 1][k]) - (win[i + 4][k] - win[i][k])) * (-COURANT / 12.0)
                dy = diff[k] * (-COURANT / 2.0)
                der[2 + c, k, at, :] = dx + 1.0 if c == 0 else dx
                der[5 + c, k, at, :] = dy + 1.0 if c == 1 else dy
                if c == 0:
                    der[0, k, at, :] = win[i + 2][k] * (-COURANT / 12.0)
                if c == 1:
                    der[1, k, at, :] = win[i + 2][k] * (-COURANT / 2.0)


def stage(src, start, der, row, count, keep, scale, put):
    masks = lane_masks()
    mid = [[[src[c, k, pl.ds(row + 8 * i, 8), :] for k in range(NK)] for i in range(count)] for c in range(2)]
    for c in range(3):
        win = [[src[c, k, pl.ds(row + 8 * i - 16, 8), :] for k in range(NK)] for i in range(count + 4)]
        for i in range(count):
            at = pl.ds(row + 8 * i, 8)
            diff = lat_difference(win[i + 2], masks)
            for k in range(NK):
                dx = 8.0 * (win[i + 3][k] - win[i + 1][k]) - (win[i + 4][k] - win[i][k])
                s = der[0, k, at, :] * dx + der[1, k, at, :] * diff[k]
                s = s + mid[0][i][k] * der[2 + c, k, at, :] + mid[1][i][k] * der[5 + c, k, at, :]
                if c == 2:
                    s = s + win[i + 2][k]
                if keep:
                    s = s + keep * start[c, k, at, :]
                if scale != 1.0:
                    s = s * scale
                put(c, k, row + 8 * i, s)


def sweep(low, high, count, body):
    rows = count * LEV

    def at(i, carry):
        body(pl.multiple_of(low + i * rows, LEV))
        return carry

    lax.fori_loop(0, (high - low) // rows, at, 0)


def choices_of(step):
    return (0, 2) if step == 0 else (0, 1, 2, 3)


def into(ref, shift=0):
    def put(c, k, row, s):
        ref[c, k, pl.ds(row + shift, LEV), :] = s

    return put


def rows_of(low, count):
    return pl.ds(low * LEV, count * LEV)


def interior_kernel(step, slots, table_ref, p_ref, *refs):
    choices = choices_of(step)
    cores = refs[: len(choices)]
    out_ref, handed_ref, base, der, two, three = refs[len(choices) :]
    _, which = timetable(table_ref, slots)
    for choice, core in zip(choices, cores):

        @pl.when(which[step] == choice)
        def _(core=core):
            for c in range(3):
                for k in range(NK):
                    base[c, k] = core[c, k].astype(F32)

    sweep(2 * LEV, 30 * LEV, RUN[0], lambda row: derive(base, der, row, RUN[0]))

    def vector(v, carry):
        one = p_ref.at[v]
        last = into(out_ref.at[v])
        sweep(2 * LEV, 30 * LEV, RUN[1], lambda row: stage(one, one, der, row, RUN[1], 0.0, 1.0, into(two)))
        sweep(4 * LEV, 28 * LEV, RUN[2], lambda row: stage(two, one, der, row, RUN[2], 3.0, 1.0, into(three)))
        sweep(6 * LEV, 26 * LEV, RUN[3], lambda row: stage(three, one, der, row, RUN[3], 2.0, 1.0 / 6.0, last))
        for c in range(3):
            for k in range(NK):
                for i, (held, places) in enumerate(zip((two, three), HANDED)):
                    for side, (low, _) in enumerate(places):
                        handed_ref[v, c, k, rows_of(8 * i + 4 * side, 4), :] = held[c, k, rows_of(low, 4), :]
        return carry

    lax.fori_loop(0, p_ref.shape[0], vector, 0)


def interior(step, slots, table, pert, cores):
    nv = pert.shape[0]
    args = [table, pert, *cores]
    field = pltpu.VMEM((3, NK, CORE, LANES), F32)
    return pl.pallas_call(
        functools.partial(interior_kernel, step, slots),
        in_specs=[pl.BlockSpec(memory_space=pltpu.SMEM)] + [pl.BlockSpec(memory_space=pltpu.VMEM)] * (len(args) - 1),
        out_specs=[pl.BlockSpec(memory_space=pltpu.VMEM)] * 2,
        out_shape=[
            jax.ShapeDtypeStruct((nv, 3, NK, CORE, LANES), F32),
            jax.ShapeDtypeStruct((nv, 3, NK, 16 * LEV, LANES), F32),
        ],
        scratch_shapes=[field, pltpu.VMEM((8, NK, CORE, LANES), F32), field, field],
        compiler_params=pltpu.CompilerParams(vmem_limit_bytes=VMEM_LIMIT),
        cost_estimate=pl.CostEstimate(flops=INTERIOR_FLOPS, bytes_accessed=100_000, transcendentals=0),
        name="interior",
    )(*args)


def boundary_kernel(step, slots, last, *refs):
    table_ref, p_ref, inner_ref, handed_ref, left_ref, right_ref, own_a, own_b, own_left, own_right = refs[:10]
    sets = [(0, own_a, own_left.at[0], own_right.at[0]), (1, own_b, own_left.at[1], own_right.at[1])]
    taken = 10
    for choice in (2, 3) if step else (2,):
        sets.append((choice, *refs[taken : taken + 3]))
        taken += 3
    rest = refs[taken:]
    if last:
        order_ref, out_ref, base, der, one, two, three, whole = rest
    else:
        out_ref, head_ref, tail_ref, base, der, one, two, three = rest
    _, which = timetable(table_ref, slots)
    for choice, core, left, right in sets:

        @pl.when(which[step] == choice)
        def _(core=core, left=left, right=right):
            for c in range(3):
                for k in range(NK):
                    base[0, c, k, rows_of(0, 6), :] = left[c, k].astype(F32)
                    base[0, c, k, rows_of(6, 10), :] = core[c, k, rows_of(0, 10), :].astype(F32)
                    base[1, c, k, rows_of(0, 10), :] = core[c, k, rows_of(22, 10), :].astype(F32)
                    base[1, c, k, rows_of(10, 6), :] = right[c, k].astype(F32)

    for side, low in enumerate((2, 4)):
        sweep(low * LEV, (low + 10) * LEV, 10, lambda row, side=side: derive(base.at[side], der.at[side], row, 10))

    def vector(v, carry):
        for c in range(3):
            for k in range(NK):
                one[0, c, k, rows_of(6, 10), :] = p_ref[v, c, k, rows_of(0, 10), :]
                high = left_ref[v, c, k, pl.ds(0, RIM), :].astype(F32)
                rest = left_ref[v, c, k, pl.ds(RIM, NEAR), :].astype(F32)
                one[0, c, k, pl.ds(0, RIM - NEAR), :] = high[: RIM - NEAR]
                one[0, c, k, pl.ds(RIM - NEAR, NEAR), :] = high[RIM - NEAR :] + rest
                one[1, c, k, rows_of(0, 10), :] = p_ref[v, c, k, rows_of(22, 10), :]
                high = right_ref[v, c, k, pl.ds(0, RIM), :].astype(F32)
                rest = right_ref[v, c, k, pl.ds(RIM, NEAR), :].astype(F32)
                one[1, c, k, pl.ds(10 * LEV, NEAR), :] = high[:NEAR] + rest
                one[1, c, k, pl.ds(10 * LEV + NEAR, RIM - NEAR), :] = high[NEAR:]
                for i, (held, places) in enumerate(zip((two, three), HANDED)):
                    for side, (_, low) in enumerate(places):
                        held[side, c, k, rows_of(low, 4), :] = handed_ref[v, c, k, rows_of(8 * i + 4 * side, 4), :]
        final = whole if last else out_ref.at[v]
        for side, low in enumerate((2, 8)):
            stage(one.at[side], one.at[side], der.at[side], low * LEV, 6, 0.0, 1.0, into(two.at[side]))
        for side, low in enumerate((4, 6)):
            stage(two.at[side], one.at[side], der.at[side], low * LEV, 6, 3.0, 1.0, into(three.at[side]))
        for side, (low, shift) in enumerate(((6, -6), (4, 22))):
            put = into(final, shift * LEV)
            stage(three.at[side], one.at[side], der.at[side], low * LEV, 6, 2.0, 1.0 / 6.0, put)
        for c in range(3):
            for k in range(NK):
                final[c, k, rows_of(6, 20), :] = inner_ref[v, c, k, rows_of(6, 20), :]
            if last:
                out_ref[v, c] = split_dot(gather_rows(whole.at[c]), order_ref[...]).reshape(LEV, LON, NLAT)
            else:
                pack_edges(out_ref.at[v, c], head_ref.at[v], tail_ref.at[v], (c,))
        return carry

    lax.fori_loop(0, p_ref.shape[0], vector, 0)


def boundary(step, slots, table, pert, inner, edges, bases, order):
    last = step == STEPS - 1
    nv = pert.shape[0]
    args = [table, pert, *inner, *edges, *bases]
    side = pltpu.VMEM((2, 3, NK, SIDE, LANES), F32)
    scratch = [side, pltpu.VMEM((2, 8, NK, SIDE, LANES), F32), side, side, side]
    if last:
        args.append(order)
        scratch.append(pltpu.VMEM((3, NK, CORE, LANES), F32))
        out_shape = jax.ShapeDtypeStruct((nv, 3, LEV, LON, NLAT), F32)
        out_specs = pl.BlockSpec(memory_space=pltpu.VMEM)
    else:
        out_shape = [
            jax.ShapeDtypeStruct((nv, 3, NK, CORE, LANES), F32),
            jax.ShapeDtypeStruct((nv, 3, NK, RIM + NEAR, LANES), BF16),
            jax.ShapeDtypeStruct((nv, 3, NK, RIM + NEAR, LANES), BF16),
        ]
        out_specs = [pl.BlockSpec(memory_space=pltpu.VMEM)] * 3
    return pl.pallas_call(
        functools.partial(boundary_kernel, step, slots, last),
        in_specs=[pl.BlockSpec(memory_space=pltpu.SMEM)] + [pl.BlockSpec(memory_space=pltpu.VMEM)] * (len(args) - 1),
        out_specs=out_specs,
        out_shape=out_shape,
        scratch_shapes=scratch,
        compiler_params=pltpu.CompilerParams(vmem_limit_bytes=VMEM_LIMIT),
        cost_estimate=pl.CostEstimate(flops=1_000_000, bytes_accessed=100_000, transcendentals=0),
        name="last_boundary" if last else "boundary",
    )(*args)


def neighbours(head, tail):
    count = lax.axis_size("tile")
    left = lax.ppermute(tail, "tile", [(i, (i + 1) % count) for i in range(count)])
    right = lax.ppermute(head, "tile", [((i + 1) % count, i) for i in range(count)])
    return left, right


def on_device(order, order_back, vectors, trajectory, slot_table):
    slots = trajectory.shape[0]
    swap = [(0, 1), (1, 0)]
    own_a, own_b, head, tail = convert_base(slot_table, trajectory)
    got = [lax.ppermute(core, "member", swap) for core in (own_a, own_b)]
    own = (own_a, own_b, *neighbours(head, tail))

    def with_halo(core):
        return core, *neighbours(core[:, :, :RIM], core[:, :, CORE - RIM :])

    got[0] = with_halo(got[0])
    pert, head, tail = convert_vectors(vectors, order)
    for step in range(STEPS):
        edges = neighbours(head, tail)
        cores = (own_a, own_b, got[0][0], got[1][0] if step else None)
        inner = interior(step, slots, slot_table, pert, [cores[i] for i in choices_of(step)])
        bases = (*own, *got[0], *got[1]) if step else (*own, *got[0])
        done = boundary(step, slots, slot_table, pert, inner, edges, bases, order_back)
        if step == STEPS - 1:
            return done
        pert, head, tail = done
        if step == 0:
            pert, second = lax.optimization_barrier((pert, got[1]))
            got[1] = with_halo(second)


def solution(mesh):
    order = lane_order()

    def program(vectors, trajectory, slot_table):
        body = functools.partial(on_device, jnp.asarray(order, BF16), jnp.asarray(order.T, BF16))
        spec = P("member", None, None, "tile", None)
        return jax.shard_map(body, mesh=mesh, in_specs=(spec, spec, P()), out_specs=spec, check_vma=False)(
            vectors, trajectory, slot_table
        )

    return program
```
